32 devices in a mesh: groups: 2 (over y), tensor: 4 (over z), dp: 2 (over x), pipe: 2 (over core).
Axes of the slice: x: 2, y: 2, z: 4, core: 2. Of those that a mesh axis runs over, the one named last changes fastest.
Arguments:
- residual_input: bfloat16 [512, 8192], P(('groups', 'dp'), 'tensor'), parts along dimension 0, may hold values from -6 to 6
- norm_gain_layers: float32 [2, 8192], replicated, may hold values from 0.25 to 1.75
- query_projection_weight: bfloat16 [2, 8192, 8192], P('pipe', 'dp', 'tensor'), may hold values from -0.0625 to 0.0625
- output_projection_weight: bfloat16 [2, 8192, 8192], P('pipe', 'tensor', 'dp'), may hold values from -0.0625 to 0.0625
- query_down_maps: bfloat16 [2, 8, 8192, 64], P('pipe', None, None, 'tensor'), may hold values from -0.0625 to 0.0625
- query_up_maps: bfloat16 [2, 8, 64, 8192], P('pipe', None, None, 'tensor'), may hold values from -0.75 to 0.75
- output_down_maps: bfloat16 [2, 8, 8192, 64], P('pipe', None, 'tensor'), may hold values from -0.0625 to 0.0625
- output_up_maps: bfloat16 [2, 8, 64, 8192], P('pipe', None, None, 'tensor'), may hold values from -0.75 to 0.75
- keyval_cache: bfloat16 [2, 512, 8, 16, 256], P('pipe', ('groups', 'dp'), 'tensor'), parts along dimension 1, may hold values from -120 to 120, as said below
- token_keyval: bfloat16 [2, 512, 8, 256], P('pipe', ('groups', 'dp'), 'tensor'), parts along dimension 1, may hold values from -4 to 4, as said below
- row_adapter_index: int32 [512], P(('groups', 'dp')), parts along dimension 0, may hold values from 0 to 7
- cache_length: int32 [512], P(('groups', 'dp')), parts along dimension 0, may hold values from 1 to 16, as said below
Outputs:
- hidden_out: bfloat16 [512, 8192], P(('groups', 'dp', 'pipe'), 'tensor'), parts along dimension 0
The draws below stay inside these ranges and needn't reach their ends.
There are 2 independent parts, one for each index of `groups`. The reference program is written for one: setup_inputs(seed, part) draws one part's arguments, and reference() takes and returns one part's arrays. A program takes and returns all parts, laid end to end along the dimension named above; an argument that names none is the same for every part. Nothing has to cross between parts.
Inputs may be any that keep to these rules, and one draw needn't show every extreme that they name: `cache_length`: some row has all 16 positions valid and some row has one. `keyval_cache`: slot s is a copy of key-value head s * 1: slots of the same key-value head are equal. `token_keyval`: slot s is a copy of key-value head s * 1: slots of the same key-value head are equal.
All inputs are finite; a program needn't handle non-finite values.
Results may differ from the reference program's by a relative error of at most 0.028.
Values may be sent and summed in bfloat16 or wider, within the bound.
A program may use at most 256 MiB of HBM per device.

```python
import math
import jax
import jax.numpy as jnp
from jax import lax

MODEL_WIDTH = 8192
HEADS = 64
KV_HEADS = 8
HD = 128
ADAPTER_RANK = 64
ADAPTER_COUNT = 8
LEN = 16
LAYER_COUNT = 2
QUERY_FEATURES = 8192
SHARD_Q = 2048
SLOTS = 8
TOKENS = 256


def row_lengths(key):
    key = jax.random.fold_in(key, 7)
    lengths = jax.random.randint(key, (TOKENS,), 1, LEN + 1, dtype=jnp.int32)
    lengths = lengths.at[0].set(LEN)
    return lengths.at[1].set(1)


def spread_slots(heads):
    return jnp.repeat(heads, SLOTS // KV_HEADS, axis=2)


def draw_cache_length(key, part):
    return row_lengths(key)


def draw_keyval_cache(key, part):
    lengths = row_lengths(key)
    key = jax.random.fold_in(key, 11)
    streams = jax.random.split(key, 6)
    shape = (LAYER_COUNT, TOKENS, KV_HEADS, LEN, 2 * HD)
    base = jnp.clip(jax.random.normal(streams[0], shape, jnp.float32), -4.0, 4.0)
    share = 0.125
    chosen = jax.random.uniform(streams[1], (LAYER_COUNT, TOKENS, KV_HEADS), jnp.float32) < share
    chosen = chosen.at[:, 0, :].set(True)
    position = jnp.arange(LEN, dtype=jnp.int32)
    spots = jax.random.uniform(streams[2], (LAYER_COUNT, TOKENS, KV_HEADS, LEN), jnp.float32) < 0.4
    first_row = (jnp.arange(TOKENS, dtype=jnp.int32) == 0)[None, :, None, None]
    spots = spots | (position < 2)[None, None, None, :] & first_row
    spots = spots & (position[None, :] < lengths[:, None])[None, :, None, :]
    planted = chosen[..., None] & spots
    strength = jnp.exp(jax.random.uniform(streams[3], (LAYER_COUNT, TOKENS, KV_HEADS), jnp.float32, math.log(40.0), math.log(120.0)))
    strength = strength.at[:, 0, 0].set(120.0)
    signs = jnp.where(jax.random.uniform(streams[4], (LAYER_COUNT, TOKENS, KV_HEADS, 1, HD), jnp.float32) < 0.5, -1.0, 1.0)
    jitter = jnp.clip(0.5 * jax.random.normal(streams[5], (LAYER_COUNT, TOKENS, KV_HEADS, LEN, HD), jnp.float32), -2.0, 2.0)
    aligned = jnp.clip(strength[..., None, None] * signs + jitter, -120.0, 120.0)
    key_part = jnp.where(planted[..., None], aligned, base[..., :HD])
    heads = jnp.concatenate([key_part, base[..., HD:]], axis=-1)
    return spread_slots(heads).astype(jnp.bfloat16)


def draw_token_keyval(key, part):
    key = jax.random.fold_in(key, 13)
    shape = (LAYER_COUNT, TOKENS, KV_HEADS, 2 * HD)
    heads = jnp.clip(jax.random.normal(key, shape, jnp.float32), -4.0, 4.0)
    return spread_slots(heads).astype(jnp.bfloat16)


def place_ends(drawn, rng, smallest, top_value):
    place = [jax.random.randint(jax.random.fold_in(rng, axis), (), 0, length) for axis, length in enumerate(drawn.shape)]
    longest = drawn.shape.index(max(drawn.shape))
    beside = place[:longest] + [(place[longest] + 1) % drawn.shape[longest]] + place[longest + 1:]
    return drawn.at[tuple(place)].set(smallest).at[tuple(beside)].set(top_value)


def block_levels(stream_key, shape, cuts, least, largest):
    gain = 1.0
    for dim, parts in cuts:
        draws = jax.random.uniform(jax.random.fold_in(jax.random.fold_in(stream_key, 6), dim), (parts,), jnp.float32, least / len(cuts), largest / len(cuts))
        gain = gain * jnp.repeat(jnp.exp(draws), shape[dim] // parts).reshape((-1,) + (1,) * (len(shape) - 1 - dim))
    return gain


def scatter_about(rng, extent, scale, most, cuts=(), kind=jnp.bfloat16):
    level = block_levels(rng, extent, cuts, -0.22, 0.18) if cuts else 1.0
    result = jax.random.normal(rng, extent, jnp.float32) * scale * level
    return jnp.minimum(jnp.maximum(result, -most), most).astype(kind)


def setup_inputs(seed: int = 0, part: int = 0) -> dict:
    streams_of = jax.random.split(jax.random.key(seed), 13)
    part_splits = jax.random.split(jax.random.fold_in(streams_of[12], part), 13)
    return {
        "residual_input": scatter_about(part_splits[0], (TOKENS, MODEL_WIDTH), 1.0, 6.0, ((0, 2), (1, 4))),
        "norm_gain_layers": jnp.clip(1.0 + 0.15 * jax.random.normal(streams_of[1], (LAYER_COUNT, MODEL_WIDTH), jnp.float32), 0.25, 1.75),
        "query_projection_weight": scatter_about(streams_of[2], (LAYER_COUNT, MODEL_WIDTH, QUERY_FEATURES), MODEL_WIDTH ** -0.5, 0.0625, ((0, 2), (1, 2), (2, 4))),
        "output_projection_weight": scatter_about(streams_of[3], (LAYER_COUNT, QUERY_FEATURES, MODEL_WIDTH), QUERY_FEATURES ** -0.5, 0.0625, ((0, 2), (1, 4), (2, 2))),
        "query_down_maps": scatter_about(streams_of[4], (LAYER_COUNT, ADAPTER_COUNT, MODEL_WIDTH, ADAPTER_RANK), MODEL_WIDTH ** -0.5, 0.0625, ((0, 2), (3, 4))),
        "query_up_maps": scatter_about(streams_of[5], (LAYER_COUNT, ADAPTER_COUNT, ADAPTER_RANK, QUERY_FEATURES), ADAPTER_RANK ** -0.5, 0.75, ((0, 2), (3, 4))),
        "output_down_maps": scatter_about(streams_of[6], (LAYER_COUNT, ADAPTER_COUNT, QUERY_FEATURES, ADAPTER_RANK), QUERY_FEATURES ** -0.5, 0.0625, ((0, 2), (2, 4))),
        "output_up_maps": scatter_about(streams_of[7], (LAYER_COUNT, ADAPTER_COUNT, ADAPTER_RANK, MODEL_WIDTH), ADAPTER_RANK ** -0.5, 0.75, ((0, 2), (3, 4))),
        "keyval_cache": draw_keyval_cache(jax.random.fold_in(jax.random.fold_in(streams_of[12], part), 71), part),
        "token_keyval": draw_token_keyval(jax.random.fold_in(jax.random.fold_in(streams_of[12], part), 71), part),
        "row_adapter_index": place_ends(jax.random.randint(part_splits[10], (TOKENS,), 0, ADAPTER_COUNT), jax.random.fold_in(part_splits[10], 1), 0, ADAPTER_COUNT - 1).astype(jnp.int32),
        "cache_length": draw_cache_length(jax.random.fold_in(jax.random.fold_in(streams_of[12], part), 71), part),
    }


EPSILON = 1e-05
ADAPTER_SCALE = 2.0

def widen_rank(adapter_selector, rank_vec):
    spread = adapter_selector[:, :, None] * rank_vec.astype(jnp.float32)[:, None, :]
    return spread.reshape(spread.shape[0], -1).astype(jnp.bfloat16)

def reference(residual_input, norm_gain_layers, query_projection_weight, output_projection_weight, query_down_maps, query_up_maps, output_down_maps, output_up_maps, keyval_cache, token_keyval, row_adapter_index, cache_length):
    hidden_state = residual_input
    count = hidden_state.shape[0]
    adapter_selector = (row_adapter_index[:, None] == jnp.arange(ADAPTER_COUNT, dtype=jnp.int32)[None, :]).astype(jnp.float32)
    inv_scale = HD ** (-0.5)
    per_slot = HEADS // SLOTS
    slice_width = SHARD_Q
    valid_mask = (jnp.arange(LEN, dtype=jnp.int32)[None, :] < cache_length[:, None])[:, None, None, :]
    for layer_number in range(LAYER_COUNT):
        hidden_single = hidden_state.astype(jnp.float32)
        mean_sq = lax.optimization_barrier(jnp.mean(hidden_single * hidden_single, axis=-1, keepdims=True))
        normed_state = (hidden_single * lax.rsqrt(mean_sq + EPSILON) * norm_gain_layers[layer_number]).astype(jnp.bfloat16)
        rank_every_query = jnp.einsum('iq,gqh->igh', normed_state.astype(jnp.float32), query_down_maps[layer_number].astype(jnp.float32))
        query_rank_state = lax.optimization_barrier(jnp.sum(adapter_selector[:, :, None] * rank_every_query, axis=1)).astype(jnp.bfloat16)
        query_state = jnp.dot(normed_state, query_projection_weight[layer_number], preferred_element_type=jnp.float32)
        query_state = query_state + ADAPTER_SCALE * jnp.dot(widen_rank(adapter_selector, query_rank_state), query_up_maps[layer_number].reshape(ADAPTER_COUNT * ADAPTER_RANK, QUERY_FEATURES), preferred_element_type=jnp.float32)
        query_state = query_state.astype(jnp.bfloat16).reshape(count, SLOTS, per_slot, HD).astype(jnp.float32)
        layer_cache = keyval_cache[layer_number].astype(jnp.float32)
        cache_keys = layer_cache[..., :HD]
        cache_vals = layer_cache[..., HD:]
        newest_keyval = token_keyval[layer_number].astype(jnp.float32)
        new_key = newest_keyval[..., :HD]
        new_val = newest_keyval[..., HD:]
        scores = jnp.einsum('nshd,nsld->nshl', query_state, cache_keys) * inv_scale
        new_score = jnp.einsum('nshd,nsd->nsh', query_state, new_key) * inv_scale
        row_max = jnp.maximum(lax.optimization_barrier(jnp.max(jnp.where(valid_mask, scores, -1e+30), axis=-1)), new_score)
        exp_cache = jnp.where(valid_mask, jnp.exp(scores - row_max[..., None]), 0.0)
        exp_new = jnp.exp(new_score - row_max)
        totals = lax.optimization_barrier(jnp.sum(exp_cache, axis=-1)) + exp_new
        prob_cache = (exp_cache / totals[..., None]).astype(jnp.bfloat16).astype(jnp.float32)
        prob_new = (exp_new / totals).astype(jnp.bfloat16).astype(jnp.float32)
        attention_result = jnp.einsum('nshl,nsld->nshd', prob_cache, cache_vals) + prob_new[..., None] * new_val[:, :, None, :]
        attention_result = attention_result.astype(jnp.bfloat16).reshape(count, QUERY_FEATURES)
        plain_output = jnp.zeros((count, MODEL_WIDTH), jnp.float32)
        for shard_index in range(QUERY_FEATURES // slice_width):
            lower = shard_index * slice_width
            partial_value = jnp.dot(attention_result[:, lower:lower + slice_width], output_projection_weight[layer_number][lower:lower + slice_width, :], preferred_element_type=jnp.float32)
            partial_value = lax.optimization_barrier(partial_value.astype(jnp.bfloat16))
            plain_output = plain_output + partial_value.astype(jnp.float32)
        rank_every_output = jnp.einsum('cb,dbm->cdm', attention_result.astype(jnp.float32), output_down_maps[layer_number].astype(jnp.float32))
        output_rank_state = lax.optimization_barrier(jnp.sum(adapter_selector[:, :, None] * rank_every_output, axis=1)).astype(jnp.bfloat16)
        adapter_result = jnp.dot(widen_rank(adapter_selector, output_rank_state), output_up_maps[layer_number].reshape(ADAPTER_COUNT * ADAPTER_RANK, MODEL_WIDTH), preferred_element_type=jnp.float32)
        hidden_state = (hidden_single + plain_output + ADAPTER_SCALE * adapter_result).astype(jnp.bfloat16)
    return hidden_state
```

```python
import functools

import jax
import jax.numpy as jnp
from jax import lax
from jax.experimental import pallas as pl
from jax.experimental.pallas import tpu as pltpu
from jax.sharding import PartitionSpec as P

EPSILON = 1e-05
ADAPTER_SCALE = 2.0


def shifted(block, axis, distance):
    devices = range(lax.axis_size(axis))
    route = [(i - distance, i) for i in devices if i - distance in devices]
    return lax.ppermute(block, axis, route)


def widen_rank(adapter_selector, rank_vec):
    spread = adapter_selector[:, :, None] * rank_vec.astype(jnp.float32)[:, None, :]
    return spread.reshape(spread.shape[0], -1).astype(jnp.bfloat16)


def attend(queries, layer_cache, newest_keyval, row_valid_length):
    head_dim = queries.shape[-1]
    inv_scale = head_dim ** (-0.5)
    cache_keys = layer_cache[..., :head_dim]
    cache_vals = layer_cache[..., head_dim:]
    new_key = newest_keyval[..., :head_dim]
    new_val = newest_keyval[..., head_dim:]
    valid_mask = (
        jnp.arange(layer_cache.shape[2], dtype=jnp.int32)[None, :] < row_valid_length[:, None]
    )[:, None, None, :]
    scores = (
        jnp.einsum("nshd,nsld->nshl", queries, cache_keys, preferred_element_type=jnp.float32)
        * inv_scale
    )
    new_score = (
        jnp.einsum("nshd,nsd->nsh", queries, new_key, preferred_element_type=jnp.float32)
        * inv_scale
    )
    row_max = jnp.maximum(jnp.max(jnp.where(valid_mask, scores, -1e30), axis=-1), new_score)
    exp_cache = jnp.where(valid_mask, jnp.exp(scores - row_max[..., None]), 0.0)
    exp_new = jnp.exp(new_score - row_max)
    totals = jnp.sum(exp_cache, axis=-1) + exp_new
    prob_cache = (exp_cache / totals[..., None]).astype(jnp.bfloat16)
    prob_new = (exp_new / totals).astype(jnp.bfloat16)
    attention_result = jnp.einsum(
        "nshl,nsld->nshd", prob_cache, cache_vals, preferred_element_type=jnp.float32
    )
    attention_result = (
        attention_result
        + prob_new.astype(jnp.float32)[..., None] * new_val.astype(jnp.float32)[:, :, None, :]
    )
    return attention_result.astype(jnp.bfloat16)


def run_layer(
    incoming_state,
    layer_row_gain,
    query_matrix,
    adapter_group,
    row_adapter_picks,
    row_valid_length,
    layer_cache,
    newest_keyval,
    output_pieces,
):
    query_down_picked, query_up_picked, output_down_picked, output_up_picked = adapter_group
    adapters = query_down_picked.shape[0]
    rank = query_up_picked.shape[1]
    micro_rows = incoming_state.shape[0]
    head_dim = layer_cache.shape[-1] // 2
    slot_count = layer_cache.shape[1]
    gathered = lax.all_gather(incoming_state, "tensor", axis=1, tiled=True)
    hidden_single = gathered.astype(jnp.float32)
    mean_sq = jnp.mean(hidden_single * hidden_single, axis=-1, keepdims=True)
    normed_state = (hidden_single * lax.rsqrt(mean_sq + EPSILON) * layer_row_gain).astype(
        jnp.bfloat16
    )
    adapter_selector = (
        row_adapter_picks[:, None] == jnp.arange(adapters, dtype=jnp.int32)[None, :]
    ).astype(jnp.float32)
    rank_every_query = jnp.einsum(
        "iq,gqh->igh", normed_state, query_down_picked, preferred_element_type=jnp.float32
    )
    rank_local = jnp.sum(adapter_selector[:, :, None] * rank_every_query, axis=1).astype(
        jnp.bfloat16
    )
    query_rank_state = lax.all_gather(rank_local, "tensor", axis=1, tiled=True)
    plain_query = jnp.dot(normed_state, query_matrix, preferred_element_type=jnp.float32)
    query_state = plain_query + ADAPTER_SCALE * jnp.dot(
        widen_rank(adapter_selector, query_rank_state),
        query_up_picked.reshape(adapters * rank, -1),
        preferred_element_type=jnp.float32,
    )
    query_state = query_state.astype(jnp.bfloat16).reshape(micro_rows, slot_count, -1, head_dim)
    attention_result = attend(query_state, layer_cache, newest_keyval, row_valid_length).reshape(
        micro_rows, -1
    )
    plain_output = lax.psum_scatter(
        output_pieces(attention_result).astype(jnp.bfloat16),
        "tensor",
        scatter_dimension=1,
        tiled=True,
    ).astype(jnp.float32)
    rank_every_output = jnp.einsum(
        "cb,dbm->cdm", attention_result, output_down_picked, preferred_element_type=jnp.float32
    )
    rank_part = jnp.sum(adapter_selector[:, :, None] * rank_every_output, axis=1)
    output_rank_state = lax.psum(rank_part, "tensor").astype(jnp.bfloat16)
    adapter_result = jnp.dot(
        widen_rank(adapter_selector, output_rank_state),
        output_up_picked.reshape(adapters * rank, -1),
        preferred_element_type=jnp.float32,
    )
    return (
        incoming_state.astype(jnp.float32) + plain_output + ADAPTER_SCALE * adapter_result
    ).astype(jnp.bfloat16)


def body(
    residual_input,
    norm_gain_layers,
    query_projection_weight,
    output_projection_weight,
    query_down_maps,
    query_up_maps,
    output_down_maps,
    output_up_maps,
    keyval_cache,
    token_keyval,
    row_adapter_index,
    cache_length,
):
    section_index = lax.axis_index("pipe")
    micro_rows = residual_input.shape[0] // 2
    layer_groups = (
        query_projection_weight,
        output_projection_weight,
        query_down_maps,
        query_up_maps,
        output_down_maps,
        output_up_maps,
    )
    query_sets = lax.all_gather(layer_groups[0], "dp", axis=1, tiled=True)
    output_full = lax.all_gather(layer_groups[1][0], "dp", axis=1, tiled=True)
    adapter_group = tuple((adapter_member[0] for adapter_member in layer_groups[2:]))
    layer_row_gain = lax.dynamic_index_in_dim(norm_gain_layers, section_index, 0, keepdims=False)

    def output_pieces(attention_result):
        return jnp.dot(attention_result, output_full, preferred_element_type=jnp.float32)

    section_out = jnp.zeros((micro_rows, residual_input.shape[1]), jnp.bfloat16)
    first_out = section_out
    for tick_step in range(3):
        if tick_step > 0:
            passed = shifted(section_out, "pipe", 1)
        else:
            passed = section_out
        micro_block = jnp.clip(tick_step - section_index, 0, 1)
        row_start = micro_block * micro_rows
        own_rows = lax.dynamic_slice_in_dim(residual_input, row_start, micro_rows, 0)
        incoming_state = jnp.where(section_index == 0, own_rows, passed)
        row_adapter_picks = lax.dynamic_slice_in_dim(row_adapter_index, row_start, micro_rows, 0)
        row_valid_length = lax.dynamic_slice_in_dim(cache_length, row_start, micro_rows, 0)
        layer_cache = lax.dynamic_slice_in_dim(keyval_cache[0], row_start, micro_rows, 0)
        newest_keyval = lax.dynamic_slice_in_dim(token_keyval[0], row_start, micro_rows, 0)
        section_out = run_layer(
            incoming_state,
            layer_row_gain,
            query_sets[0],
            adapter_group,
            row_adapter_picks,
            row_valid_length,
            layer_cache,
            newest_keyval,
            output_pieces,
        )
        if tick_step == 1:
            first_out = section_out
    returned = shifted(first_out, "pipe", -1)
    result = jnp.where(section_index == 0, returned, section_out)
    return result


MESH = pl.DeviceIdType.MESH


def comm_call(kernel, outs, scratch, collective_id, *args):
    vmem = pl.BlockSpec(memory_space=pltpu.VMEM)
    return pl.pallas_call(
        kernel,
        out_shape=outs,
        in_specs=[vmem] * len(args),
        out_specs=jax.tree.map(lambda _: vmem, outs),
        scratch_shapes=scratch,
        compiler_params=pltpu.CompilerParams(
            collective_id=collective_id, has_side_effects=True, vmem_limit_bytes=48 * 2**20
        ),
    )(*args)


def greet(*targets):
    barrier = pltpu.get_barrier_semaphore()
    for target in targets:
        pl.semaphore_signal(barrier, inc=1, device_id=target, device_id_type=MESH)
    pl.semaphore_wait(barrier, len(targets))


def remote(src, dst, send, recv, target):
    return pltpu.make_async_remote_copy(
        src_ref=src, dst_ref=dst, send_sem=send, recv_sem=recv, device_id=target, device_id_type=MESH
    )


def z_neighbours(k, tensor):
    return [{"tensor": j} for j in (k - 1, k + 1) if 0 <= j < tensor]


def gather_kernel(active, tensor, chunks, h_ref, own_ref, other_ref, zs, zr, xs, xr):
    d, t, p = lax.axis_index("dp"), lax.axis_index("tensor"), lax.axis_index("pipe")
    rows = h_ref.shape[0] // chunks
    half = tensor // 2

    @pl.when(p == active)
    def _():
        for k in range(tensor):

            @pl.when(t == k)
            def _(k=k):
                greet({"dp": 1 - d}, *z_neighbours(k, tensor))
                order = sorted(range(tensor), key=lambda s: abs(s - k))

                def hop(s, c, dest):
                    part = pl.ds(c * rows, rows)
                    src = h_ref.at[part] if s == k else own_ref.at[s, part]
                    way = 0 if dest > k else 1
                    return remote(
                        src, own_ref.at[s, part], zs.at[way, s, c], zr.at[s, c], {"tensor": dest}
                    )

                def across(s, c):
                    part = pl.ds(c * rows, rows)
                    src = h_ref.at[part] if s == k else own_ref.at[s, part]
                    return remote(
                        src, other_ref.at[s % half, part], xs.at[s, c], xr.at[s % half, c], {"dp": 1 - d}
                    )

                def arrived(s, c):
                    part = pl.ds(c * rows, rows)
                    view = own_ref.at[s, part]
                    remote(view, view, zs.at[0, s, c], zr.at[s, c], {"dp": 1 - d}).wait_recv()

                def dests(s):
                    up = [k + 1] if s <= k and k + 1 < tensor else []
                    down = [k - 1] if s >= k and k > 0 else []
                    return up + down

                for s in order:
                    for c in range(chunks):
                        if s != k:
                            arrived(s, c)
                        for dest in dests(s):
                            hop(s, c, dest).start()

                        @pl.when(s // half != d)
                        def _(s=s, c=c):
                            across(s, c).start()
                    if s == k:
                        own_ref[k] = h_ref[...]
                for s in range(tensor):
                    for c in range(chunks):
                        for dest in dests(s):
                            hop(s, c, dest).wait_send()

                        @pl.when(s // half != d)
                        def _(s=s, c=c):
                            across(s, c).wait_send()
                for j in range(half):
                    for c in range(chunks):
                        view = other_ref.at[j, pl.ds(c * rows, rows)]
                        remote(view, view, xs.at[j, c], xr.at[j, c], {"dp": 1 - d}).wait_recv()


def gather_rows(h, active, collective_id, tensor):
    rows, cols = h.shape
    chunks = 4
    dma = pltpu.SemaphoreType.DMA
    return comm_call(
        functools.partial(gather_kernel, active, tensor, chunks),
        (
            jax.ShapeDtypeStruct((tensor, rows, cols), h.dtype),
            jax.ShapeDtypeStruct((tensor // 2, rows, cols), h.dtype),
        ),
        [dma((2, tensor, chunks)), dma((tensor, chunks)), dma((tensor, chunks)), dma((tensor // 2, chunks))],
        collective_id,
        h,
    )


def exchange_kernel(active, tensor, blk_ref, small_ref, rblk_ref, rsmall_ref, bs, br, ss, sr):
    d, t, p = lax.axis_index("dp"), lax.axis_index("tensor"), lax.axis_index("pipe")
    count = 2 * tensor
    me = d * tensor + t

    def place(off):
        target = lax.rem(me + off, count)
        return target // tensor, lax.rem(target, tensor)

    @pl.when(p == active)
    def _():
        greet(*[{"dp": place(off)[0], "tensor": place(off)[1]} for off in range(1, count)])
        big = remote(blk_ref, rblk_ref, bs, br, {"dp": 1 - d})
        copies = []
        for off in range(1, count):
            d2, t2 = place(off)
            copies.append(
                remote(
                    small_ref.at[d2],
                    rsmall_ref.at[d, t],
                    ss.at[off],
                    sr.at[off],
                    {"dp": d2, "tensor": t2},
                )
            )
        for copy in copies:
            copy.start()
        big.start()
        rsmall_ref[d, t] = small_ref[d]
        for copy in copies:
            copy.wait()
        big.wait()


def exchange(block, small, active, collective_id, tensor):
    dma = pltpu.SemaphoreType.DMA
    return comm_call(
        functools.partial(exchange_kernel, active, tensor),
        (
            jax.ShapeDtypeStruct(block.shape, block.dtype),
            jax.ShapeDtypeStruct((2, tensor) + small.shape[1:], small.dtype),
        ),
        [dma, dma, dma((2 * tensor,)), dma((2 * tensor,))],
        collective_id,
        block,
        small,
    )


def reduce_kernel(active, tensor, p_ref, h_ref, out_ref, up, dn, su, sd, us, ur, ds, dr, cs, cr):
    t, p = lax.axis_index("tensor"), lax.axis_index("pipe")
    chunks = p_ref.shape[0]

    def to_core(c):
        return remote(out_ref.at[c], out_ref.at[c], cs.at[c], cr.at[c], {"pipe": 1 - p})

    @pl.when(p != active)
    def _():
        greet({"pipe": 1 - p})
        for c in range(chunks):
            to_core(c).wait_recv()

    @pl.when(p == active)
    def _():
        for k in range(tensor):

            @pl.when(t == k)
            def _(k=k):
                greet({"pipe": 1 - p}, *z_neighbours(k, tensor))
                last = tensor - 1

                def send_up(c, src):
                    return remote(src.at[c], up.at[c], us.at[c], ur.at[c], {"tensor": k + 1})

                def send_dn(c, src):
                    return remote(src.at[c], dn.at[c], ds.at[c], dr.at[c], {"tensor": k - 1})

                def f32(ref, c):
                    return ref[c].astype(jnp.float32)

                def up_step(c):
                    remote(up.at[c], up.at[c], us.at[c], ur.at[c], {"pipe": 1 - p}).wait_recv()
                    if k < last:
                        su[c] = (f32(p_ref, c) + f32(up, c)).astype(su.dtype)
                        send_up(c, su).start()

                def dn_step(c):
                    remote(dn.at[c], dn.at[c], ds.at[c], dr.at[c], {"pipe": 1 - p}).wait_recv()
                    if k > 0:
                        sd[c] = (f32(p_ref, c) + f32(dn, c)).astype(sd.dtype)
                        send_dn(c, sd).start()

                def finish(c):
                    total = f32(h_ref, c) + f32(p_ref, c)
                    if k > 0:
                        total = total + f32(up, c)
                    if k < last:
                        total = total + f32(dn, c)
                    out_ref[c] = total.astype(out_ref.dtype)
                    to_core(c).start()

                lag_up = max(0, 2 * k - last) if 0 < k < last else 0
                lag_dn = max(0, last - 2 * k) if 0 < k < last else 0

                if k == 0 or k == last:

                    @pl.loop(0, chunks)
                    def _(c):
                        (send_up if k == 0 else send_dn)(c, p_ref).start()

                for i in range(chunks + max(lag_up, lag_dn)):
                    cu, cd = i - lag_up, i - lag_dn
                    if k > 0 and 0 <= cu < chunks:
                        up_step(cu)
                    if k < last and 0 <= cd < chunks:
                        dn_step(cd)
                    done = i - max(lag_up, lag_dn)
                    if done >= 0:
                        finish(done)

                @pl.loop(0, chunks)
                def _(c):
                    if k < last:
                        send_up(c, p_ref if k == 0 else su).wait_send()
                    if k > 0:
                        send_dn(c, p_ref if k == last else sd).wait_send()
                    to_core(c).wait_send()


def reduce_rows(partial, h, active, collective_id, tensor):
    rows, cols = partial.shape
    chunks = 16
    shape = (chunks, rows // chunks, cols)
    dma = pltpu.SemaphoreType.DMA((chunks,))
    buffer = pltpu.VMEM(shape, partial.dtype)
    return comm_call(
        functools.partial(reduce_kernel, active, tensor),
        jax.ShapeDtypeStruct(shape, partial.dtype),
        [buffer] * 4 + [dma] * 6,
        collective_id,
        partial.reshape(shape),
        h.reshape(shape),
    ).reshape(rows, cols)


def scatter_kernel(
    active, tensor, p_ref, out_ref, xb, up, dn, su, sd, res, xs, xr, us, ur, ds, dr, cs, cr
):
    d, t, p = lax.axis_index("dp"), lax.axis_index("tensor"), lax.axis_index("pipe")
    half, chunks = p_ref.shape[1], p_ref.shape[2]
    mine = chunks // 2
    last = tensor - 1

    def core_copy(c):
        return remote(res.at[c], out_ref.at[c], cs.at[c], cr.at[c], {"pipe": 1 - p})

    @pl.when(p != active)
    def _():
        greet({"pipe": 1 - p})
        for c in range(mine):
            core_copy(c).wait_recv()

    @pl.when(p == active)
    def _():
        for k in range(tensor):

            @pl.when(t == k)
            def _(k=k):
                greet({"pipe": 1 - p}, {"dp": 1 - d}, *z_neighbours(k, tensor))

                def cross(j, c):
                    return remote(
                        p_ref.at[1 - d, j, c], xb.at[j, c], xs.at[j, c], xr.at[j, c], {"dp": 1 - d}
                    )

                def send_up(s, c):
                    return remote(su.at[s, c], up.at[s, c], us.at[s, c], ur.at[s, c], {"tensor": k + 1})

                def send_dn(s, c):
                    return remote(sd.at[s, c], dn.at[s, c], ds.at[s, c], dr.at[s, c], {"tensor": k - 1})

                def own(s, c):
                    return jnp.where(
                        d == s // half, p_ref[d, s % half, c], xb[s % half, c]
                    ).astype(jnp.float32)

                for c in range(chunks):
                    for j in range(half):
                        cross(j, c).start()

                for c in range(chunks):
                    for j in range(half):
                        cross(j, c).wait_recv()
                    for s in range(last, k, -1):
                        total = own(s, c)
                        if k > 0:
                            send_up(s, c).wait_recv()
                            total = total + up[s, c].astype(jnp.float32)
                        su[s, c] = total.astype(su.dtype)
                        send_up(s, c).start()
                    for s in range(k):
                        total = own(s, c)
                        if k < last:
                            send_dn(s, c).wait_recv()
                            total = total + dn[s, c].astype(jnp.float32)
                        sd[s, c] = total.astype(sd.dtype)
                        send_dn(s, c).start()
                for c in range(chunks):
                    total = own(k, c)
                    if k > 0:
                        send_up(k, c).wait_recv()
                        total = total + up[k, c].astype(jnp.float32)
                    if k < last:
                        send_dn(k, c).wait_recv()
                        total = total + dn[k, c].astype(jnp.float32)
                    if c < mine:
                        res[c] = total.astype(res.dtype)
                        core_copy(c).start()
                    else:
                        out_ref[c - mine] = total.astype(out_ref.dtype)
                for c in range(chunks):
                    for j in range(half):
                        cross(j, c).wait_send()
                    for s in range(k + 1, tensor):
                        send_up(s, c).wait_send()
                    for s in range(k):
                        send_dn(s, c).wait_send()
                for c in range(mine):
                    core_copy(c).wait_send()


def scatter_rows(partial, active, collective_id, tensor):
    _, rows, half, cols = partial.shape
    chunks = 4
    part = rows // chunks
    blocks = jnp.transpose(partial.reshape(2, chunks, part, half, cols), (0, 3, 1, 2, 4))
    dma = pltpu.SemaphoreType.DMA
    line = pltpu.VMEM((tensor, chunks, part, cols), partial.dtype)
    return comm_call(
        functools.partial(scatter_kernel, active, tensor),
        jax.ShapeDtypeStruct((chunks // 2, part, cols), partial.dtype),
        [pltpu.VMEM((half, chunks, part, cols), partial.dtype)]
        + [line] * 4
        + [pltpu.VMEM((chunks // 2, part, cols), partial.dtype)]
        + [dma((half, chunks))] * 2
        + [dma((tensor, chunks))] * 4
        + [dma((chunks // 2,))] * 2,
        collective_id,
        blocks,
    ).reshape(rows // 2, cols)


def fast_layer(act, gain, weights, adapter_index, lengths, cache, newest, active, ids, tensor):
    wq, wo, q_down, q_up, o_down, o_up = weights
    d, t = lax.axis_index("dp"), lax.axis_index("tensor")
    rows, k_half = act.shape[1:]
    adapters, rank = q_up.shape[0], q_up.shape[1]
    rank_local = q_down.shape[2]
    head_dim, slots = cache.shape[-1] // 2, cache.shape[1]
    features = k_half * 2

    act32 = act.astype(jnp.float32)
    gain_half = lax.dynamic_slice_in_dim(gain, d * k_half, k_half, 0)
    scaled = (act32 * gain_half).astype(jnp.bfloat16).reshape(2 * rows, k_half)
    squares = jnp.sum(act32 * act32, axis=-1)
    partial = jnp.dot(scaled, wq, preferred_element_type=jnp.float32).reshape(2, rows, -1)
    down_half = lax.dynamic_slice_in_dim(q_down, d * k_half, k_half, 1)
    ranks = jnp.einsum("nk,akr->arn", scaled, down_half, preferred_element_type=jnp.float32)
    ranks = jnp.transpose(ranks.reshape(adapters * rank_local, 2, rows), (1, 0, 2))
    index_row = jnp.broadcast_to(adapter_index.astype(jnp.float32), (2, 1, rows))
    small = jnp.concatenate([ranks, squares[:, None], index_row], axis=1)
    small = jnp.pad(small, ((0, 0), (0, -small.shape[1] % 8), (0, 0)))
    sent = lax.dynamic_index_in_dim(partial, 1 - d, 0, keepdims=False).astype(jnp.bfloat16)
    came, smalls = exchange(sent, small, active, ids[0], tensor)
    own = lax.dynamic_index_in_dim(partial, d, 0, keepdims=False)
    width = adapters * rank_local
    squares_all = smalls[0, 0, width] + smalls[1, 0, width]
    factor = lax.rsqrt(squares_all / features + EPSILON)
    selector = (adapter_index[:, None] == jnp.arange(adapters, dtype=jnp.int32)[None, :]).astype(jnp.float32)
    rank_sum = (smalls[0, :, :width] + smalls[1, :, :width]).reshape(tensor, adapters, rank_local, rows)
    rank_vec = jnp.einsum("tarn,na->ntr", rank_sum, selector * factor[:, None], precision=lax.Precision.HIGHEST)
    rank_vec = rank_vec.reshape(rows, rank).astype(jnp.bfloat16)
    query = (own + came.astype(jnp.float32)) * factor[:, None] + ADAPTER_SCALE * jnp.dot(
        widen_rank(selector, rank_vec),
        q_up.reshape(adapters * rank, -1),
        preferred_element_type=jnp.float32,
    )
    query = query.astype(jnp.bfloat16).reshape(rows, slots, -1, head_dim)
    attended = attend(query, cache, newest, lengths).reshape(rows, -1)

    rank_every = jnp.einsum("cb,dbm->cdm", attended, o_down, preferred_element_type=jnp.float32)
    rank_part = jnp.sum(selector[:, :, None] * rank_every, axis=1).T
    came, rank_parts = exchange(
        attended, jnp.broadcast_to(rank_part, (2,) + rank_part.shape), active, ids[1], tensor
    )
    first = jnp.where(d == 0, attended, came)
    second = jnp.where(d == 0, came, attended)
    both = jnp.concatenate([first, second], axis=0)
    partial = jnp.dot(both, wo, preferred_element_type=jnp.float32)
    rank_all = jnp.transpose(jnp.sum(rank_parts, axis=1), (0, 2, 1)).reshape(2 * rows, rank).astype(jnp.bfloat16)
    index_all = smalls[:, 0, width + 1].reshape(2 * rows)
    selector_all = (index_all[:, None] == jnp.arange(adapters, dtype=jnp.float32)[None, :]).astype(jnp.float32)
    delta = ADAPTER_SCALE * jnp.dot(
        widen_rank(selector_all, rank_all), o_up.reshape(adapters * rank, -1), preferred_element_type=jnp.float32
    )
    return partial.reshape(2 * rows, tensor // 2, -1), delta


def fast_body(
    residual_input, norm_gain, wq, wo, q_down, q_up, o_down, o_up, cache, newest, adapter_index, lengths
):
    tensor = lax.axis_size("tensor")
    half = tensor // 2
    d, t, p = lax.axis_index("dp"), lax.axis_index("tensor"), lax.axis_index("pipe")
    rows, cols = residual_input.shape
    weights = tuple(w[0] for w in (wq, wo, q_down, q_up, o_down, o_up))
    gain = lax.dynamic_index_in_dim(norm_gain, p, 0, keepdims=False)
    here = (jnp.arange(half) + d * half == t)[None, :, None]

    own, other = gather_rows(residual_input, 0, 0, tensor)
    mine = lax.dynamic_slice_in_dim(own, d * half, half, 0)
    first = jnp.where(d == 0, mine, other)
    second = jnp.where(d == 0, other, mine)
    act = jnp.transpose(jnp.stack([first, second]), (0, 2, 1, 3)).reshape(2, rows, half * cols)

    def layer(act, active, ids):
        return fast_layer(
            act, gain, weights, adapter_index, lengths, cache[0], newest[0], active, ids, tensor
        )

    partial, delta = layer(act, 0, (1, 2))
    partial = jnp.where(here, partial + delta[:, None, :], partial).astype(jnp.bfloat16)
    act = reduce_rows(
        partial.reshape(2 * rows, half * cols), act.reshape(2 * rows, half * cols), 0, 3, tensor
    )
    act = act.reshape(2, rows, half * cols)
    partial, delta = layer(act, 1, (4, 5))
    residual = act.reshape(2 * rows, half, cols).astype(jnp.float32)
    partial = jnp.where(here, partial + delta[:, None, :] + residual, partial).astype(jnp.bfloat16)
    return scatter_rows(partial.reshape(2, rows, half, cols), 1, 6, tensor)


SPECS = (
    P(("groups", "dp"), "tensor"),
    P(),
    P("pipe", "dp", "tensor"),
    P("pipe", "tensor", "dp"),
    P("pipe", None, None, "tensor"),
    P("pipe", None, None, "tensor"),
    P("pipe", None, "tensor", None),
    P("pipe", None, None, "tensor"),
    P("pipe", ("groups", "dp"), "tensor", None, None),
    P("pipe", ("groups", "dp"), "tensor", None),
    P(("groups", "dp")),
    P(("groups", "dp")),
)


def solution(mesh):
    small = mesh.shape["dp"] == 2 and mesh.shape["tensor"] == 4 and mesh.shape["pipe"] == 2
    return jax.shard_map(
        fast_body if small else body,
        mesh=mesh,
        in_specs=SPECS,
        out_specs=P(("groups", "dp", "pipe"), "tensor"),
        check_vma=False,
    )
```

```python
import functools

import jax
import jax.numpy as jnp
from jax import lax
from jax.experimental import pallas as pl
from jax.experimental.pallas import tpu as pltpu
from jax.sharding import PartitionSpec as P

EPSILON = 1e-05
ADAPTER_SCALE = 2.0


def shifted(block, axis, distance):
    devices = range(lax.axis_size(axis))
    route = [(i - distance, i) for i in devices if i - distance in devices]
    return lax.ppermute(block, axis, route)


def widen_rank(adapter_selector, rank_vec):
    spread = adapter_selector[:, :, None] * rank_vec.astype(jnp.float32)[:, None, :]
    return spread.reshape(spread.shape[0], -1).astype(jnp.bfloat16)


def attend(queries, layer_cache, newest_keyval, row_valid_length):
    head_dim = queries.shape[-1]
    inv_scale = head_dim ** (-0.5)
    cache_keys = layer_cache[..., :head_dim]
    cache_vals = layer_cache[..., head_dim:]
    new_key = newest_keyval[..., :head_dim]
    new_val = newest_keyval[..., head_dim:]
    valid_mask = (
        jnp.arange(layer_cache.shape[2], dtype=jnp.int32)[None, :] < row_valid_length[:, None]
    )[:, None, None, :]
    scores = (
        jnp.einsum("nshd,nsld->nshl", queries, cache_keys, preferred_element_type=jnp.float32)
        * inv_scale
    )
    new_score = (
        jnp.einsum("nshd,nsd->nsh", queries, new_key, preferred_element_type=jnp.float32)
        * inv_scale
    )
    row_max = jnp.maximum(jnp.max(jnp.where(valid_mask, scores, -1e30), axis=-1), new_score)
    exp_cache = jnp.where(valid_mask, jnp.exp(scores - row_max[..., None]), 0.0)
    exp_new = jnp.exp(new_score - row_max)
    totals = jnp.sum(exp_cache, axis=-1) + exp_new
    prob_cache = (exp_cache / totals[..., None]).astype(jnp.bfloat16)
    prob_new = (exp_new / totals).astype(jnp.bfloat16)
    attention_result = jnp.einsum(
        "nshl,nsld->nshd", prob_cache, cache_vals, preferred_element_type=jnp.float32
    )
    attention_result = (
        attention_result
        + prob_new.astype(jnp.float32)[..., None] * new_val.astype(jnp.float32)[:, :, None, :]
    )
    return attention_result.astype(jnp.bfloat16)


def run_layer(
    incoming_state,
    layer_row_gain,
    query_matrix,
    adapter_group,
    row_adapter_picks,
    row_valid_length,
    layer_cache,
    newest_keyval,
    output_pieces,
):
    query_down_picked, query_up_picked, output_down_picked, output_up_picked = adapter_group
    adapters = query_down_picked.shape[0]
    rank = query_up_picked.shape[1]
    micro_rows = incoming_state.shape[0]
    head_dim = layer_cache.shape[-1] // 2
    slot_count = layer_cache.shape[1]
    gathered = lax.all_gather(incoming_state, "tensor", axis=1, tiled=True)
    hidden_single = gathered.astype(jnp.float32)
    mean_sq = jnp.mean(hidden_single * hidden_single, axis=-1, keepdims=True)
    normed_state = (hidden_single * lax.rsqrt(mean_sq + EPSILON) * layer_row_gain).astype(
        jnp.bfloat16
    )
    adapter_selector = (
        row_adapter_picks[:, None] == jnp.arange(adapters, dtype=jnp.int32)[None, :]
    ).astype(jnp.float32)
    rank_every_query = jnp.einsum(
        "iq,gqh->igh", normed_state, query_down_picked, preferred_element_type=jnp.float32
    )
    rank_local = jnp.sum(adapter_selector[:, :, None] * rank_every_query, axis=1).astype(
        jnp.bfloat16
    )
    query_rank_state = lax.all_gather(rank_local, "tensor", axis=1, tiled=True)
    plain_query = jnp.dot(normed_state, query_matrix, preferred_element_type=jnp.float32)
    query_state = plain_query + ADAPTER_SCALE * jnp.dot(
        widen_rank(adapter_selector, query_rank_state),
        query_up_picked.reshape(adapters * rank, -1),
        preferred_element_type=jnp.float32,
    )
    query_state = query_state.astype(jnp.bfloat16).reshape(micro_rows, slot_count, -1, head_dim)
    attention_result = attend(query_state, layer_cache, newest_keyval, row_valid_length).reshape(
        micro_rows, -1
    )
    plain_output = lax.psum_scatter(
        output_pieces(attention_result).astype(jnp.bfloat16),
        "tensor",
        scatter_dimension=1,
        tiled=True,
    ).astype(jnp.float32)
    rank_every_output = jnp.einsum(
        "cb,dbm->cdm", attention_result, output_down_picked, preferred_element_type=jnp.float32
    )
    rank_part = jnp.sum(adapter_selector[:, :, None] * rank_every_output, axis=1)
    output_rank_state = lax.psum(rank_part, "tensor").astype(jnp.bfloat16)
    adapter_result = jnp.dot(
        widen_rank(adapter_selector, output_rank_state),
        output_up_picked.reshape(adapters * rank, -1),
        preferred_element_type=jnp.float32,
    )
    return (
        incoming_state.astype(jnp.float32) + plain_output + ADAPTER_SCALE * adapter_result
    ).astype(jnp.bfloat16)


def body(
    residual_input,
    norm_gain_layers,
    query_projection_weight,
    output_projection_weight,
    query_down_maps,
    query_up_maps,
    output_down_maps,
    output_up_maps,
    keyval_cache,
    token_keyval,
    row_adapter_index,
    cache_length,
):
    section_index = lax.axis_index("pipe")
    micro_rows = residual_input.shape[0] // 2
    layer_groups = (
        query_projection_weight,
        output_projection_weight,
        query_down_maps,
        query_up_maps,
        output_down_maps,
        output_up_maps,
    )
    query_sets = lax.all_gather(layer_groups[0], "dp", axis=1, tiled=True)
    output_full = lax.all_gather(layer_groups[1][0], "dp", axis=1, tiled=True)
    adapter_group = tuple((adapter_member[0] for adapter_member in layer_groups[2:]))
    layer_row_gain = lax.dynamic_index_in_dim(norm_gain_layers, section_index, 0, keepdims=False)

    def output_pieces(attention_result):
        return jnp.dot(attention_result, output_full, preferred_element_type=jnp.float32)

    section_out = jnp.zeros((micro_rows, residual_input.shape[1]), jnp.bfloat16)
    first_out = section_out
    for tick_step in range(3):
        if tick_step > 0:
            passed = shifted(section_out, "pipe", 1)
        else:
            passed = section_out
        micro_block = jnp.clip(tick_step - section_index, 0, 1)
        row_start = micro_block * micro_rows
        own_rows = lax.dynamic_slice_in_dim(residual_input, row_start, micro_rows, 0)
        incoming_state = jnp.where(section_index == 0, own_rows, passed)
        row_adapter_picks = lax.dynamic_slice_in_dim(row_adapter_index, row_start, micro_rows, 0)
        row_valid_length = lax.dynamic_slice_in_dim(cache_length, row_start, micro_rows, 0)
        layer_cache = lax.dynamic_slice_in_dim(keyval_cache[0], row_start, micro_rows, 0)
        newest_keyval = lax.dynamic_slice_in_dim(token_keyval[0], row_start, micro_rows, 0)
        section_out = run_layer(
            incoming_state,
            layer_row_gain,
            query_sets[0],
            adapter_group,
            row_adapter_picks,
            row_valid_length,
            layer_cache,
            newest_keyval,
            output_pieces,
        )
        if tick_step == 1:
            first_out = section_out
    returned = shifted(first_out, "pipe", -1)
    result = jnp.where(section_index == 0, returned, section_out)
    return result


MESH = pl.DeviceIdType.MESH


def comm_call(kernel, outs, scratch, collective_id, *args):
    vmem = pl.BlockSpec(memory_space=pltpu.VMEM)
    return pl.pallas_call(
        kernel,
        out_shape=outs,
        in_specs=[vmem] * len(args),
        out_specs=jax.tree.map(lambda _: vmem, outs),
        scratch_shapes=scratch,
        compiler_params=pltpu.CompilerParams(
            collective_id=collective_id, has_side_effects=True, vmem_limit_bytes=48 * 2**20
        ),
    )(*args)


def greet(*targets):
    barrier = pltpu.get_barrier_semaphore()
    for target in targets:
        pl.semaphore_signal(barrier, inc=1, device_id=target, device_id_type=MESH)
    pl.semaphore_wait(barrier, len(targets))


def remote(src, dst, send, recv, target):
    return pltpu.make_async_remote_copy(
        src_ref=src, dst_ref=dst, send_sem=send, recv_sem=recv, device_id=target, device_id_type=MESH
    )


def z_neighbours(k, tensor):
    return [{"tensor": j} for j in (k - 1, k + 1) if 0 <= j < tensor]


def gather_kernel(
    active, tensor, chunks, h_ref, index_ref, own_ref, other_ref, rindex_ref, zs, zr, xs, xr, js, jr
):
    d, t, p = lax.axis_index("dp"), lax.axis_index("tensor"), lax.axis_index("pipe")
    rows = h_ref.shape[0] // chunks
    half = tensor // 2

    def index_copy():
        return remote(index_ref, rindex_ref, js, jr, {"dp": 1 - d})

    @pl.when(p != active)
    def _():
        greet({"dp": 1 - d})
        index_copy().start()
        index_copy().wait()

    @pl.when(p == active)
    def _():
        for k in range(tensor):

            @pl.when(t == k)
            def _(k=k):
                greet({"dp": 1 - d}, *z_neighbours(k, tensor))
                index_copy().start()
                order = sorted(range(tensor), key=lambda s: abs(s - k))

                def hop(s, c, dest):
                    part = pl.ds(c * rows, rows)
                    src = h_ref.at[part] if s == k else own_ref.at[s, part]
                    way = 0 if dest > k else 1
                    return remote(
                        src, own_ref.at[s, part], zs.at[way, s, c], zr.at[s, c], {"tensor": dest}
                    )

                def across(s, c):
                    part = pl.ds(c * rows, rows)
                    src = h_ref.at[part] if s == k else own_ref.at[s, part]
                    return remote(
                        src, other_ref.at[s % half, part], xs.at[s, c], xr.at[s % half, c], {"dp": 1 - d}
                    )

                def arrived(s, c):
                    part = pl.ds(c * rows, rows)
                    view = own_ref.at[s, part]
                    remote(view, view, zs.at[0, s, c], zr.at[s, c], {"dp": 1 - d}).wait_recv()

                def dests(s):
                    up = [k + 1] if s <= k and k + 1 < tensor else []
                    down = [k - 1] if s >= k and k > 0 else []
                    return up + down

                for s in order:
                    for c in range(chunks):
                        if s != k:
                            arrived(s, c)
                        for dest in dests(s):
                            hop(s, c, dest).start()

                        @pl.when(s // half != d)
                        def _(s=s, c=c):
                            across(s, c).start()
                    if s == k:
                        own_ref[k] = h_ref[...]
                for s in range(tensor):
                    for c in range(chunks):
                        for dest in dests(s):
                            hop(s, c, dest).wait_send()

                        @pl.when(s // half != d)
                        def _(s=s, c=c):
                            across(s, c).wait_send()
                for j in range(half):
                    for c in range(chunks):
                        view = other_ref.at[j, pl.ds(c * rows, rows)]
                        remote(view, view, xs.at[j, c], xr.at[j, c], {"dp": 1 - d}).wait_recv()
                index_copy().wait()


def gather_rows(h, index, active, collective_id, tensor):
    rows, cols = h.shape
    chunks = 4
    dma = pltpu.SemaphoreType.DMA
    return comm_call(
        functools.partial(gather_kernel, active, tensor, chunks),
        (
            jax.ShapeDtypeStruct((tensor, rows, cols), h.dtype),
            jax.ShapeDtypeStruct((tensor // 2, rows, cols), h.dtype),
            jax.ShapeDtypeStruct(index.shape, index.dtype),
        ),
        [dma((2, tensor, chunks)), dma((tensor, chunks)), dma((tensor, chunks)), dma((tensor // 2, chunks))]
        + [dma, dma],
        collective_id,
        h,
        index,
    )


PIECES = 4


def exchange_kernel(active, tensor, narrow, blk_ref, small_ref, rblk_ref, rsmall_ref, bs, br, ss, sr):
    d, t, p = lax.axis_index("dp"), lax.axis_index("tensor"), lax.axis_index("pipe")
    count = 2 * tensor
    half = tensor // 2
    me = d * tensor + t
    size = blk_ref.shape[0] // PIECES

    def place(off):
        target = lax.rem(me + off, count)
        return target // tensor, lax.rem(target, tensor)

    @pl.when(p == active)
    def _():
        greet(*[{"dp": place(off)[0], "tensor": place(off)[1]} for off in range(1, count)])
        big = []
        for i in range(PIECES):
            part = pl.ds(i * size, size)
            big.append(remote(blk_ref.at[part], rblk_ref.at[part], bs.at[i], br.at[i], {"dp": 1 - d}))

        def small_copy(off):
            d2, t2 = place(off)
            src = small_ref.at[0] if narrow else small_ref.at[d2]
            return remote(src, rsmall_ref.at[d, t], ss.at[off], sr.at[off], {"dp": d2, "tensor": t2})

        def wanted(off):
            d2, t2 = place(off)
            return t2 // half == d2

        for off in range(1, count):
            if narrow:
                pl.when(wanted(off))(lambda off=off: small_copy(off).start())
            else:
                small_copy(off).start()
        for copy in big:
            copy.start()
        rsmall_ref[d, t] = small_ref[0] if narrow else small_ref[d]
        for off in range(1, count):
            if narrow:
                pl.when(wanted(off))(lambda off=off: small_copy(off).wait_send())
                pl.when(t // half == d)(lambda off=off: small_copy(off).wait_recv())
            else:
                small_copy(off).wait()
        for copy in big:
            copy.wait()


def exchange(block, small, active, collective_id, tensor, narrow):
    dma = pltpu.SemaphoreType.DMA
    return comm_call(
        functools.partial(exchange_kernel, active, tensor, narrow),
        (
            jax.ShapeDtypeStruct(block.shape, block.dtype),
            jax.ShapeDtypeStruct((2, tensor) + small.shape[1:], small.dtype),
        ),
        [dma((PIECES,)), dma((PIECES,)), dma((2 * tensor,)), dma((2 * tensor,))],
        collective_id,
        block,
        small,
    )


WINDOW = 4


def reduce_kernel(active, tensor, splits, p_ref, h_ref, out_ref, up, dn, su, sd, us, ur, ds, dr, cs, cr):
    t, p = lax.axis_index("tensor"), lax.axis_index("pipe")
    chunks = p_ref.shape[0] // 16 * splits
    cols = p_ref.shape[1] // splits
    last = tensor - 1

    def at(ref, c):
        return ref.at[pl.ds(c // splits * 16, 16), pl.ds(c % splits * cols, cols)]

    def f32(ref, c):
        return at(ref, c)[...].astype(jnp.float32)

    def to_core(c):
        return remote(at(out_ref, c), at(out_ref, c), cs.at[c], cr.at[c], {"pipe": 1 - p})

    @pl.when(p != active)
    def _():
        greet({"pipe": 1 - p})
        for c in range(chunks):
            to_core(c).wait_recv()

    @pl.when(p == active)
    def _():
        for k in range(tensor):

            @pl.when(t == k)
            def _(k=k):
                greet({"pipe": 1 - p}, *z_neighbours(k, tensor))

                def send_up(c):
                    src = p_ref if k == 0 else su
                    return remote(at(src, c), at(up, c), us.at[c], ur.at[c], {"tensor": k + 1})

                def send_dn(c):
                    src = p_ref if k == last else sd
                    return remote(at(src, c), at(dn, c), ds.at[c], dr.at[c], {"tensor": k - 1})

                def step(c, source, out, summed, send, recv_sem):
                    if source:
                        buf = up if summed is su else dn
                        remote(at(buf, c), at(buf, c), us.at[c], recv_sem.at[c], {"pipe": 1 - p}).wait_recv()
                    if out:
                        if source:
                            at(summed, c)[...] = (f32(p_ref, c) + f32(buf, c)).astype(summed.dtype)
                        if c >= WINDOW:
                            send(c - WINDOW).wait_send()
                        send(c).start()

                def finish(c):
                    total = f32(h_ref, c) + f32(p_ref, c)
                    if k > 0:
                        total = total + f32(up, c)
                    if k < last:
                        total = total + f32(dn, c)
                    at(out_ref, c)[...] = total.astype(out_ref.dtype)
                    to_core(c).start()

                lag_up, lag_dn = k, last - k
                for i in range(chunks + max(lag_up, lag_dn)):
                    cu, cd, done = i - lag_up, i - lag_dn, i - max(lag_up, lag_dn)
                    if 0 <= cu < chunks:
                        step(cu, k > 0, k < last, su, send_up, ur)
                    if 0 <= cd < chunks:
                        step(cd, k < last, k > 0, sd, send_dn, dr)
                    if done >= 0:
                        finish(done)
                for c in range(chunks):
                    if c >= chunks - WINDOW:
                        if k < last:
                            send_up(c).wait_send()
                        if k > 0:
                            send_dn(c).wait_send()
                    to_core(c).wait_send()


def reduce_rows(partial, h, active, collective_id, tensor):
    splits = 2
    dma = pltpu.SemaphoreType.DMA((partial.shape[0] // 16 * splits,))
    return comm_call(
        functools.partial(reduce_kernel, active, tensor, splits),
        jax.ShapeDtypeStruct(partial.shape, partial.dtype),
        [pltpu.VMEM(partial.shape, partial.dtype)] * 4 + [dma] * 6,
        collective_id,
        partial,
        h,
    )


def scatter_kernel(
    active, tensor, p_ref, out_ref, xb, up, dn, su, sd, res, xs, xr, us, ur, ds, dr, cs, cr
):
    d, t, p = lax.axis_index("dp"), lax.axis_index("tensor"), lax.axis_index("pipe")
    chunks = p_ref.shape[1]
    half = tensor // 2
    cols = p_ref.shape[3] // half
    mine = chunks // 2
    last = tensor - 1

    def core_copy(c):
        return remote(res.at[c], out_ref.at[c], cs.at[c], cr.at[c], {"pipe": 1 - p})

    def cross(c):
        return remote(p_ref.at[1 - d, c], xb.at[c], xs.at[c], xr.at[c], {"dp": 1 - d})

    @pl.when(p != active)
    def _():
        greet({"pipe": 1 - p})
        for c in range(mine):
            core_copy(c).wait_recv()

    @pl.when(p == active)
    def _():
        for k in range(tensor):

            @pl.when(t == k)
            def _(k=k):
                greet({"pipe": 1 - p}, {"dp": 1 - d}, *z_neighbours(k, tensor))

                def send_up(s, c):
                    return remote(su.at[s, c], up.at[s, c], us.at[s, c], ur.at[s, c], {"tensor": k + 1})

                def send_dn(s, c):
                    return remote(sd.at[s, c], dn.at[s, c], ds.at[s, c], dr.at[s, c], {"tensor": k - 1})

                def own(s, c):
                    part = pl.ds(s % half * cols, cols)
                    return jnp.where(d == s // half, p_ref[d, c, :, part], xb[c, :, part]).astype(jnp.float32)

                def up_step(c):
                    for s in range(last, k, -1):
                        total = own(s, c)
                        if k > 0:
                            send_up(s, c).wait_recv()
                            total = total + up[s, c].astype(jnp.float32)
                        su[s, c] = total.astype(su.dtype)
                        send_up(s, c).start()

                def dn_step(c):
                    for s in range(k):
                        total = own(s, c)
                        if k < last:
                            send_dn(s, c).wait_recv()
                            total = total + dn[s, c].astype(jnp.float32)
                        sd[s, c] = total.astype(sd.dtype)
                        send_dn(s, c).start()

                def finish(c):
                    total = own(k, c)
                    if k > 0:
                        send_up(k, c).wait_recv()
                        total = total + up[k, c].astype(jnp.float32)
                    if k < last:
                        send_dn(k, c).wait_recv()
                        total = total + dn[k, c].astype(jnp.float32)
                    if c < mine:
                        res[c] = total.astype(res.dtype)
                        core_copy(c).start()
                    else:
                        out_ref[c - mine] = total.astype(out_ref.dtype)

                for c in range(2):
                    cross(c).start()
                lag_up, lag_dn = k, last - k
                for i in range(chunks + max(lag_up, lag_dn)):
                    cu, cd, done = i - lag_up, i - lag_dn, i - max(lag_up, lag_dn)
                    if i < chunks:
                        if i + 2 < chunks:
                            cross(i).wait_send()
                            cross(i + 2).start()
                        cross(i).wait_recv()
                    if 0 <= cu < chunks:
                        up_step(cu)
                    if 0 <= cd < chunks:
                        dn_step(cd)
                    if done >= 0:
                        finish(done)
                for c in range(chunks):
                    if c + 2 >= chunks:
                        cross(c).wait_send()
                    for s in range(k + 1, tensor):
                        send_up(s, c).wait_send()
                    for s in range(k):
                        send_dn(s, c).wait_send()
                for c in range(mine):
                    core_copy(c).wait_send()


def scatter_rows(partial, active, collective_id, tensor):
    part = 16
    half = tensor // 2
    chunks, cols = partial.shape[0] // 2 // part, partial.shape[1] // half
    dma = pltpu.SemaphoreType.DMA
    line = pltpu.VMEM((tensor, chunks, part, cols), partial.dtype)
    return comm_call(
        functools.partial(scatter_kernel, active, tensor),
        jax.ShapeDtypeStruct((chunks // 2, part, cols), partial.dtype),
        [pltpu.VMEM((chunks, part, half * cols), partial.dtype)]
        + [line] * 4
        + [pltpu.VMEM((chunks // 2, part, cols), partial.dtype)]
        + [dma((chunks,))] * 2
        + [dma((tensor, chunks))] * 4
        + [dma((chunks // 2,))] * 2,
        collective_id,
        partial.reshape(2, chunks, part, half * cols),
    ).reshape(-1, cols)


def fast_layer(act, gain, weights, index_all, lengths, cache, newest, active, ids, tensor):
    wq, wo, q_down, q_up, o_down, o_up = weights
    d = lax.axis_index("dp")
    all_rows, k_half = act.shape
    rows = all_rows // 2
    adapters, rank = q_up.shape[0], q_up.shape[1]
    head_dim, slots = cache.shape[-1] // 2, cache.shape[1]
    features = k_half * 2
    selector_all = (index_all[:, None] == jnp.arange(adapters, dtype=jnp.float32)[None, :]).astype(jnp.float32)
    selector = lax.dynamic_slice_in_dim(selector_all, d * rows, rows, 0)

    act32 = act.astype(jnp.float32)
    gain_half = lax.dynamic_slice_in_dim(gain, d * k_half, k_half, 0)
    scaled = (act32 * gain_half).astype(jnp.bfloat16)
    squares = jnp.sum(act32 * act32, axis=-1)
    partial = jnp.dot(scaled, wq, preferred_element_type=jnp.float32)
    down_half = lax.dynamic_slice_in_dim(q_down, d * k_half, k_half, 1)
    ranks = jnp.einsum("nk,akr->nar", scaled, down_half, preferred_element_type=jnp.float32)
    ranks = jnp.sum(selector_all[:, :, None] * ranks, axis=1)
    width = ranks.shape[1]
    small = jnp.concatenate([ranks, squares[:, None]], axis=1)
    small = jnp.pad(small, ((0, 0), (0, -small.shape[1] % 8)))
    small = jnp.transpose(small.reshape(2, rows, -1), (0, 2, 1))
    sent = lax.dynamic_slice_in_dim(partial, (1 - d) * rows, rows, 0).astype(jnp.bfloat16)
    came, smalls = exchange(sent, small, active, ids[0], tensor, False)
    own = lax.dynamic_slice_in_dim(partial, d * rows, rows, 0)
    factor = lax.rsqrt((smalls[0, 0, width] + smalls[1, 0, width]) / features + EPSILON)
    rank_vec = (smalls[0, :, :width] + smalls[1, :, :width]).reshape(rank, rows) * factor[None, :]
    rank_vec = rank_vec.T.astype(jnp.bfloat16)
    query = (own + came.astype(jnp.float32)) * factor[:, None] + ADAPTER_SCALE * jnp.dot(
        widen_rank(selector, rank_vec),
        q_up.reshape(adapters * rank, -1),
        preferred_element_type=jnp.float32,
    )
    query = query.astype(jnp.bfloat16).reshape(rows, slots, -1, head_dim)
    attended = attend(query, cache, newest, lengths).reshape(rows, -1)

    rank_every = jnp.einsum("cb,dbm->cdm", attended, o_down, preferred_element_type=jnp.float32)
    rank_part = jnp.sum(selector[:, :, None] * rank_every, axis=1).T
    came, rank_parts = exchange(attended, rank_part[None], active, ids[1], tensor, True)
    first = jnp.where(d == 0, attended, came)
    second = jnp.where(d == 0, came, attended)
    both = jnp.concatenate([first, second], axis=0)
    partial = jnp.dot(both, wo, preferred_element_type=jnp.float32)
    rank_all = jnp.transpose(jnp.sum(rank_parts, axis=1), (0, 2, 1)).reshape(2 * rows, rank).astype(jnp.bfloat16)
    delta = ADAPTER_SCALE * jnp.dot(
        widen_rank(selector_all, rank_all), o_up.reshape(adapters * rank, -1), preferred_element_type=jnp.float32
    )
    return partial, jnp.concatenate([delta] * (tensor // 2), axis=1)


def fast_body(
    residual_input, norm_gain, wq, wo, q_down, q_up, o_down, o_up, cache, newest, adapter_index, lengths
):
    tensor = lax.axis_size("tensor")
    half = tensor // 2
    d, t, p = lax.axis_index("dp"), lax.axis_index("tensor"), lax.axis_index("pipe")
    rows, cols = residual_input.shape
    weights = tuple(w[0] for w in (wq, wo, q_down, q_up, o_down, o_up))
    gain = lax.dynamic_index_in_dim(norm_gain, p, 0, keepdims=False)
    here = ((jnp.arange(half * cols) // cols + d * half) == t)[None, :]

    index = adapter_index.astype(jnp.float32)
    own, other, index_other = gather_rows(residual_input, jnp.broadcast_to(index, (8, rows)), 0, 0, tensor)
    mine = lax.dynamic_slice_in_dim(own, d * half, half, 0)
    mine = jnp.concatenate([mine[j] for j in range(half)], axis=1)
    other = jnp.concatenate([other[j] for j in range(half)], axis=1)

    def by_rows(here_rows, other_rows):
        return jnp.where(d == 0, jnp.concatenate([here_rows, other_rows]), jnp.concatenate([other_rows, here_rows]))

    act = by_rows(mine, other)
    index_all = by_rows(index, index_other[0])

    def layer(act, active, ids):
        return fast_layer(act, gain, weights, index_all, lengths, cache[0], newest[0], active, ids, tensor)

    partial, delta = layer(act, 0, (1, 2))
    partial = jnp.where(here, partial + delta, partial).astype(jnp.bfloat16)
    act = reduce_rows(partial, act, 0, 3, tensor)
    partial, delta = layer(act, 1, (4, 5))
    partial = jnp.where(here, partial + delta + act.astype(jnp.float32), partial).astype(jnp.bfloat16)
    return scatter_rows(partial, 1, 6, tensor)


SPECS = (
    P(("groups", "dp"), "tensor"),
    P(),
    P("pipe", "dp", "tensor"),
    P("pipe", "tensor", "dp"),
    P("pipe", None, None, "tensor"),
    P("pipe", None, None, "tensor"),
    P("pipe", None, "tensor", None),
    P("pipe", None, None, "tensor"),
    P("pipe", ("groups", "dp"), "tensor", None, None),
    P("pipe", ("groups", "dp"), "tensor", None),
    P(("groups", "dp")),
    P(("groups", "dp")),
)


def solution(mesh):
    small = mesh.shape["dp"] == 2 and mesh.shape["tensor"] == 4 and mesh.shape["pipe"] == 2
    return jax.shard_map(
        fast_body if small else body,
        mesh=mesh,
        in_specs=SPECS,
        out_specs=P(("groups", "dp", "pipe"), "tensor"),
        check_vma=False,
    )
```

```python
import functools

import jax
import jax.numpy as jnp
from jax import lax
from jax.experimental import pallas as pl
from jax.experimental.pallas import tpu as pltpu
from jax.sharding import PartitionSpec as P

EPSILON = 1e-05
ADAPTER_SCALE = 2.0


def shifted(block, axis, distance):
    devices = range(lax.axis_size(axis))
    route = [(i - distance, i) for i in devices if i - distance in devices]
    return lax.ppermute(block, axis, route)


def widen_rank(adapter_selector, rank_vec):
    spread = adapter_selector[:, :, None] * rank_vec.astype(jnp.float32)[:, None, :]
    return spread.reshape(spread.shape[0], -1).astype(jnp.bfloat16)


def attend(queries, layer_cache, newest_keyval, row_valid_length):
    head_dim = queries.shape[-1]
    inv_scale = head_dim ** (-0.5)
    cache_keys = layer_cache[..., :head_dim]
    cache_vals = layer_cache[..., head_dim:]
    new_key = newest_keyval[..., :head_dim]
    new_val = newest_keyval[..., head_dim:]
    valid_mask = (
        jnp.arange(layer_cache.shape[2], dtype=jnp.int32)[None, :] < row_valid_length[:, None]
    )[:, None, None, :]
    scores = (
        jnp.einsum("nshd,nsld->nshl", queries, cache_keys, preferred_element_type=jnp.float32)
        * inv_scale
    )
    new_score = (
        jnp.einsum("nshd,nsd->nsh", queries, new_key, preferred_element_type=jnp.float32)
        * inv_scale
    )
    row_max = jnp.maximum(jnp.max(jnp.where(valid_mask, scores, -1e30), axis=-1), new_score)
    exp_cache = jnp.where(valid_mask, jnp.exp(scores - row_max[..., None]), 0.0)
    exp_new = jnp.exp(new_score - row_max)
    totals = jnp.sum(exp_cache, axis=-1) + exp_new
    prob_cache = (exp_cache / totals[..., None]).astype(jnp.bfloat16)
    prob_new = (exp_new / totals).astype(jnp.bfloat16)
    attention_result = jnp.einsum(
        "nshl,nsld->nshd", prob_cache, cache_vals, preferred_element_type=jnp.float32
    )
    attention_result = (
        attention_result
        + prob_new.astype(jnp.float32)[..., None] * new_val.astype(jnp.float32)[:, :, None, :]
    )
    return attention_result.astype(jnp.bfloat16)


def run_layer(
    incoming_state,
    layer_row_gain,
    query_matrix,
    adapter_group,
    row_adapter_picks,
    row_valid_length,
    layer_cache,
    newest_keyval,
    output_pieces,
):
    query_down_picked, query_up_picked, output_down_picked, output_up_picked = adapter_group
    adapters = query_down_picked.shape[0]
    rank = query_up_picked.shape[1]
    micro_rows = incoming_state.shape[0]
    head_dim = layer_cache.shape[-1] // 2
    slot_count = layer_cache.shape[1]
    gathered = lax.all_gather(incoming_state, "tensor", axis=1, tiled=True)
    hidden_single = gathered.astype(jnp.float32)
    mean_sq = jnp.mean(hidden_single * hidden_single, axis=-1, keepdims=True)
    normed_state = (hidden_single * lax.rsqrt(mean_sq + EPSILON) * layer_row_gain).astype(
        jnp.bfloat16
    )
    adapter_selector = (
        row_adapter_picks[:, None] == jnp.arange(adapters, dtype=jnp.int32)[None, :]
    ).astype(jnp.float32)
    rank_every_query = jnp.einsum(
        "iq,gqh->igh", normed_state, query_down_picked, preferred_element_type=jnp.float32
    )
    rank_local = jnp.sum(adapter_selector[:, :, None] * rank_every_query, axis=1).astype(
        jnp.bfloat16
    )
    query_rank_state = lax.all_gather(rank_local, "tensor", axis=1, tiled=True)
    plain_query = jnp.dot(normed_state, query_matrix, preferred_element_type=jnp.float32)
    query_state = plain_query + ADAPTER_SCALE * jnp.dot(
        widen_rank(adapter_selector, query_rank_state),
        query_up_picked.reshape(adapters * rank, -1),
        preferred_element_type=jnp.float32,
    )
    query_state = query_state.astype(jnp.bfloat16).reshape(micro_rows, slot_count, -1, head_dim)
    attention_result = attend(query_state, layer_cache, newest_keyval, row_valid_length).reshape(
        micro_rows, -1
    )
    plain_output = lax.psum_scatter(
        output_pieces(attention_result).astype(jnp.bfloat16),
        "tensor",
        scatter_dimension=1,
        tiled=True,
    ).astype(jnp.float32)
    rank_every_output = jnp.einsum(
        "cb,dbm->cdm", attention_result, output_down_picked, preferred_element_type=jnp.float32
    )
    rank_part = jnp.sum(adapter_selector[:, :, None] * rank_every_output, axis=1)
    output_rank_state = lax.psum(rank_part, "tensor").astype(jnp.bfloat16)
    adapter_result = jnp.dot(
        widen_rank(adapter_selector, output_rank_state),
        output_up_picked.reshape(adapters * rank, -1),
        preferred_element_type=jnp.float32,
    )
    return (
        incoming_state.astype(jnp.float32) + plain_output + ADAPTER_SCALE * adapter_result
    ).astype(jnp.bfloat16)


def body(
    residual_input,
    norm_gain_layers,
    query_projection_weight,
    output_projection_weight,
    query_down_maps,
    query_up_maps,
    output_down_maps,
    output_up_maps,
    keyval_cache,
    token_keyval,
    row_adapter_index,
    cache_length,
):
    section_index = lax.axis_index("pipe")
    micro_rows = residual_input.shape[0] // 2
    layer_groups = (
        query_projection_weight,
        output_projection_weight,
        query_down_maps,
        query_up_maps,
        output_down_maps,
        output_up_maps,
    )
    query_sets = lax.all_gather(layer_groups[0], "dp", axis=1, tiled=True)
    output_full = lax.all_gather(layer_groups[1][0], "dp", axis=1, tiled=True)
    adapter_group = tuple((adapter_member[0] for adapter_member in layer_groups[2:]))
    layer_row_gain = lax.dynamic_index_in_dim(norm_gain_layers, section_index, 0, keepdims=False)

    def output_pieces(attention_result):
        return jnp.dot(attention_result, output_full, preferred_element_type=jnp.float32)

    section_out = jnp.zeros((micro_rows, residual_input.shape[1]), jnp.bfloat16)
    first_out = section_out
    for tick_step in range(3):
        if tick_step > 0:
            passed = shifted(section_out, "pipe", 1)
        else:
            passed = section_out
        micro_block = jnp.clip(tick_step - section_index, 0, 1)
        row_start = micro_block * micro_rows
        own_rows = lax.dynamic_slice_in_dim(residual_input, row_start, micro_rows, 0)
        incoming_state = jnp.where(section_index == 0, own_rows, passed)
        row_adapter_picks = lax.dynamic_slice_in_dim(row_adapter_index, row_start, micro_rows, 0)
        row_valid_length = lax.dynamic_slice_in_dim(cache_length, row_start, micro_rows, 0)
        layer_cache = lax.dynamic_slice_in_dim(keyval_cache[0], row_start, micro_rows, 0)
        newest_keyval = lax.dynamic_slice_in_dim(token_keyval[0], row_start, micro_rows, 0)
        section_out = run_layer(
            incoming_state,
            layer_row_gain,
            query_sets[0],
            adapter_group,
            row_adapter_picks,
            row_valid_length,
            layer_cache,
            newest_keyval,
            output_pieces,
        )
        if tick_step == 1:
            first_out = section_out
    returned = shifted(first_out, "pipe", -1)
    result = jnp.where(section_index == 0, returned, section_out)
    return result


MESH = pl.DeviceIdType.MESH


def comm_call(kernel, outs, scratch, collective_id, *args):
    vmem = pl.BlockSpec(memory_space=pltpu.VMEM)
    return pl.pallas_call(
        kernel,
        out_shape=outs,
        in_specs=[vmem] * len(args),
        out_specs=jax.tree.map(lambda _: vmem, outs),
        scratch_shapes=scratch,
        compiler_params=pltpu.CompilerParams(
            collective_id=collective_id, has_side_effects=True, vmem_limit_bytes=48 * 2**20
        ),
    )(*args)


def greet(*targets):
    barrier = pltpu.get_barrier_semaphore()
    for target in targets:
        pl.semaphore_signal(barrier, inc=1, device_id=target, device_id_type=MESH)
    pl.semaphore_wait(barrier, len(targets))


def remote(src, dst, send, recv, target):
    return pltpu.make_async_remote_copy(
        src_ref=src, dst_ref=dst, send_sem=send, recv_sem=recv, device_id=target, device_id_type=MESH
    )


def z_neighbours(k, tensor):
    return [{"tensor": j} for j in (k - 1, k + 1) if 0 <= j < tensor]


LAG = 4


def gather_kernel(
    active, tensor, chunks, h_ref, index_ref, act_ref, rindex_ref, own_ref, zs, zr, xs, xr, js, jr
):
    d, t, p = lax.axis_index("dp"), lax.axis_index("tensor"), lax.axis_index("pipe")
    rows = h_ref.shape[0] // chunks
    half = tensor // 2
    all_rows, cols = h_ref.shape

    def spot(block, j, c):
        start = pl.multiple_of(block * all_rows + c * rows, rows)
        return act_ref.at[pl.ds(start, rows), pl.ds(j * cols, cols)]

    def index_copy():
        return remote(index_ref, rindex_ref, js, jr, {"dp": 1 - d})

    @pl.when(p != active)
    def _():
        greet({"dp": 1 - d})
        index_copy().start()
        index_copy().wait()

    @pl.when(p == active)
    def _():
        for k in range(tensor):

            @pl.when(t == k)
            def _(k=k):
                greet({"dp": 1 - d}, *z_neighbours(k, tensor))
                index_copy().start()
                def hop(s, c, dest):
                    part = pl.ds(c * rows, rows)
                    src = h_ref.at[part] if s == k else own_ref.at[s, part]
                    way = 0 if dest > k else 1
                    return remote(
                        src, own_ref.at[s, part], zs.at[way, s, c], zr.at[s, c], {"tensor": dest}
                    )

                def across(s, c):
                    part = pl.ds(c * rows, rows)
                    src = h_ref.at[part] if s == k else own_ref.at[s, part]
                    return remote(
                        src, spot(d, s % half, c), xs.at[s, c], xr.at[s % half, c], {"dp": 1 - d}
                    )

                def arrived(s, c):
                    part = pl.ds(c * rows, rows)
                    view = own_ref.at[s, part]
                    remote(view, view, zs.at[0, s, c], zr.at[s, c], {"dp": 1 - d}).wait_recv()

                def dests(s):
                    up = [k + 1] if s <= k and k + 1 < tensor else []
                    down = [k - 1] if s >= k and k > 0 else []
                    return up + down

                steps = sorted(
                    (c + LAG * abs(s - k), abs(s - k), s, c) for s in range(tensor) for c in range(chunks)
                )
                for _, _, s, c in steps:
                    if s != k:
                        arrived(s, c)
                    for dest in dests(s):
                        hop(s, c, dest).start()

                    @pl.when(s // half != d)
                    def _(s=s, c=c):
                        across(s, c).start()
                for s in range(tensor):

                    @pl.when(s // half == d)
                    def _(s=s):
                        block = pl.ds(pl.multiple_of(d * all_rows, all_rows), all_rows)
                        act_ref[block, pl.ds(s % half * cols, cols)] = h_ref[...] if s == k else own_ref[s]
                for s in range(tensor):
                    for c in range(chunks):
                        for dest in dests(s):
                            hop(s, c, dest).wait_send()

                        @pl.when(s // half != d)
                        def _(s=s, c=c):
                            across(s, c).wait_send()
                for j in range(half):
                    for c in range(chunks):
                        view = spot(1 - d, j, c)
                        remote(view, view, xs.at[j, c], xr.at[j, c], {"dp": 1 - d}).wait_recv()
                index_copy().wait()


def gather_rows(h, index, active, collective_id, tensor):
    rows, cols = h.shape
    chunks = 8
    dma = pltpu.SemaphoreType.DMA
    return comm_call(
        functools.partial(gather_kernel, active, tensor, chunks),
        (
            jax.ShapeDtypeStruct((2 * rows, tensor // 2 * cols), h.dtype),
            jax.ShapeDtypeStruct(index.shape, index.dtype),
        ),
        [pltpu.VMEM((tensor, rows, cols), h.dtype)]
        + [dma((2, tensor, chunks)), dma((tensor, chunks)), dma((tensor, chunks)), dma((tensor // 2, chunks))]
        + [dma, dma],
        collective_id,
        h,
        index,
    )


PIECES = 4


def exchange_kernel(active, tensor, narrow, blk_ref, small_ref, rblk_ref, rsmall_ref, bs, br, ss, sr):
    d, t, p = lax.axis_index("dp"), lax.axis_index("tensor"), lax.axis_index("pipe")
    count = 2 * tensor
    half = tensor // 2
    me = d * tensor + t
    size = blk_ref.shape[0] // PIECES

    def place(off):
        target = lax.rem(me + off, count)
        return target // tensor, lax.rem(target, tensor)

    @pl.when(p == active)
    def _():
        greet(*[{"dp": place(off)[0], "tensor": place(off)[1]} for off in range(1, count)])
        big = []
        for i in range(PIECES):
            part = pl.ds(i * size, size)
            big.append(remote(blk_ref.at[part], rblk_ref.at[part], bs.at[i], br.at[i], {"dp": 1 - d}))

        def small_copy(off):
            d2, t2 = place(off)
            src = small_ref.at[0] if narrow else small_ref.at[d2]
            return remote(src, rsmall_ref.at[d, t], ss.at[off], sr.at[off], {"dp": d2, "tensor": t2})

        def wanted(off):
            d2, t2 = place(off)
            return t2 // half == d2

        for copy in big:
            copy.start()
        for off in range(1, count):
            if narrow:
                pl.when(wanted(off))(lambda off=off: small_copy(off).start())
            else:
                small_copy(off).start()
        rsmall_ref[d, t] = small_ref[0] if narrow else small_ref[d]
        for off in range(1, count):
            if narrow:
                pl.when(wanted(off))(lambda off=off: small_copy(off).wait_send())
                pl.when(t // half == d)(lambda off=off: small_copy(off).wait_recv())
            else:
                small_copy(off).wait()
        for copy in big:
            copy.wait()


def exchange(block, small, active, collective_id, tensor, narrow):
    dma = pltpu.SemaphoreType.DMA
    return comm_call(
        functools.partial(exchange_kernel, active, tensor, narrow),
        (
            jax.ShapeDtypeStruct(block.shape, block.dtype),
            jax.ShapeDtypeStruct((2, tensor) + small.shape[1:], small.dtype),
        ),
        [dma((PIECES,)), dma((PIECES,)), dma((2 * tensor,)), dma((2 * tensor,))],
        collective_id,
        block,
        small,
    )


WINDOW = 6


def reduce_kernel(active, tensor, splits, p_ref, h_ref, out_ref, up, dn, su, sd, us, ur, ds, dr, cs, cr):
    t, p = lax.axis_index("tensor"), lax.axis_index("pipe")
    chunks = p_ref.shape[0] // 16 * splits
    cols = p_ref.shape[1] // splits
    last = tensor - 1

    def at(ref, c):
        return ref.at[pl.ds(c // splits * 16, 16), pl.ds(c % splits * cols, cols)]

    def f32(ref, c):
        return at(ref, c)[...].astype(jnp.float32)

    def to_core(c):
        return remote(at(out_ref, c), at(out_ref, c), cs.at[c], cr.at[c], {"pipe": 1 - p})

    @pl.when(p != active)
    def _():
        greet({"pipe": 1 - p})
        for c in range(chunks):
            to_core(c).wait_recv()

    @pl.when(p == active)
    def _():
        for k in range(tensor):

            @pl.when(t == k)
            def _(k=k):
                greet({"pipe": 1 - p}, *z_neighbours(k, tensor))

                def send_up(c):
                    src = p_ref if k == 0 else su
                    return remote(at(src, c), at(up, c), us.at[c], ur.at[c], {"tensor": k + 1})

                def send_dn(c):
                    src = p_ref if k == last else sd
                    return remote(at(src, c), at(dn, c), ds.at[c], dr.at[c], {"tensor": k - 1})

                def step(c, source, out, summed, send, recv_sem):
                    if source:
                        buf = up if summed is su else dn
                        remote(at(buf, c), at(buf, c), us.at[c], recv_sem.at[c], {"pipe": 1 - p}).wait_recv()
                    if out:
                        if source:
                            at(summed, c)[...] = (f32(p_ref, c) + f32(buf, c)).astype(summed.dtype)
                        if c >= WINDOW:
                            send(c - WINDOW).wait_send()
                        send(c).start()

                def finish(c):
                    total = f32(h_ref, c) + f32(p_ref, c)
                    if k > 0:
                        total = total + f32(up, c)
                    if k < last:
                        total = total + f32(dn, c)
                    at(out_ref, c)[...] = total.astype(out_ref.dtype)
                    to_core(c).start()

                lag_up, lag_dn = LAG * k, LAG * (last - k)
                for i in range(chunks + max(lag_up, lag_dn)):
                    cu, cd, done = i - lag_up, i - lag_dn, i - max(lag_up, lag_dn)
                    if 0 <= cu < chunks:
                        step(cu, k > 0, k < last, su, send_up, ur)
                    if 0 <= cd < chunks:
                        step(cd, k < last, k > 0, sd, send_dn, dr)
                    if done >= 0:
                        finish(done)
                for c in range(chunks):
                    if c >= chunks - WINDOW:
                        if k < last:
                            send_up(c).wait_send()
                        if k > 0:
                            send_dn(c).wait_send()
                    to_core(c).wait_send()


def reduce_rows(partial, h, active, collective_id, tensor):
    splits = 2
    dma = pltpu.SemaphoreType.DMA((partial.shape[0] // 16 * splits,))
    return comm_call(
        functools.partial(reduce_kernel, active, tensor, splits),
        jax.ShapeDtypeStruct(partial.shape, partial.dtype),
        [pltpu.VMEM(partial.shape, partial.dtype)] * 4 + [dma] * 6,
        collective_id,
        partial,
        h,
    )


def scatter_kernel(
    active, tensor, p_ref, out_ref, xb, up, dn, su, sd, res, xs, xr, us, ur, ds, dr, cs, cr
):
    d, t, p = lax.axis_index("dp"), lax.axis_index("tensor"), lax.axis_index("pipe")
    chunks = p_ref.shape[1]
    half = tensor // 2
    cols = p_ref.shape[3] // half
    mine = chunks // 2
    last = tensor - 1

    def core_copy(c):
        return remote(res.at[c], out_ref.at[c], cs.at[c], cr.at[c], {"pipe": 1 - p})

    def cross(c):
        return remote(p_ref.at[1 - d, c], xb.at[c], xs.at[c], xr.at[c], {"dp": 1 - d})

    @pl.when(p != active)
    def _():
        greet({"pipe": 1 - p})
        for c in range(mine):
            core_copy(c).wait_recv()

    @pl.when(p == active)
    def _():
        for k in range(tensor):

            @pl.when(t == k)
            def _(k=k):
                greet({"pipe": 1 - p}, {"dp": 1 - d}, *z_neighbours(k, tensor))

                def send_up(s, c):
                    return remote(su.at[s, c], up.at[s, c], us.at[s, c], ur.at[s, c], {"tensor": k + 1})

                def send_dn(s, c):
                    return remote(sd.at[s, c], dn.at[s, c], ds.at[s, c], dr.at[s, c], {"tensor": k - 1})

                def own(s, c):
                    part = pl.ds(s % half * cols, cols)
                    return jnp.where(d == s // half, p_ref[d, c, :, part], xb[c, :, part]).astype(jnp.float32)

                def up_step(c):
                    for s in range(last, k, -1):
                        total = own(s, c)
                        if k > 0:
                            send_up(s, c).wait_recv()
                            total = total + up[s, c].astype(jnp.float32)
                        su[s, c] = total.astype(su.dtype)
                        send_up(s, c).start()

                def dn_step(c):
                    for s in range(k):
                        total = own(s, c)
                        if k < last:
                            send_dn(s, c).wait_recv()
                            total = total + dn[s, c].astype(jnp.float32)
                        sd[s, c] = total.astype(sd.dtype)
                        send_dn(s, c).start()

                def finish(c):
                    total = own(k, c)
                    if k > 0:
                        send_up(k, c).wait_recv()
                        total = total + up[k, c].astype(jnp.float32)
                    if k < last:
                        send_dn(k, c).wait_recv()
                        total = total + dn[k, c].astype(jnp.float32)
                    if c < mine:
                        res[c] = total.astype(res.dtype)
                        core_copy(c).start()
                    else:
                        out_ref[c - mine] = total.astype(out_ref.dtype)

                for c in range(2):
                    cross(c).start()
                lag_up, lag_dn = k, last - k
                for i in range(chunks + max(lag_up, lag_dn)):
                    cu, cd, done = i - lag_up, i - lag_dn, i - max(lag_up, lag_dn)
                    if i < chunks:
                        if i + 2 < chunks:
                            cross(i).wait_send()
                            cross(i + 2).start()
                        cross(i).wait_recv()
                    if 0 <= cu < chunks:
                        up_step(cu)
                    if 0 <= cd < chunks:
                        dn_step(cd)
                    if done >= 0:
                        finish(done)
                for c in range(chunks):
                    if c + 2 >= chunks:
                        cross(c).wait_send()
                    for s in range(k + 1, tensor):
                        send_up(s, c).wait_send()
                    for s in range(k):
                        send_dn(s, c).wait_send()
                for c in range(mine):
                    core_copy(c).wait_send()


def scatter_rows(partial, active, collective_id, tensor):
    part = 16
    half = tensor // 2
    chunks, cols = partial.shape[0] // 2 // part, partial.shape[1] // half
    dma = pltpu.SemaphoreType.DMA
    line = pltpu.VMEM((tensor, chunks, part, cols), partial.dtype)
    return comm_call(
        functools.partial(scatter_kernel, active, tensor),
        jax.ShapeDtypeStruct((chunks // 2, part, cols), partial.dtype),
        [pltpu.VMEM((chunks, part, half * cols), partial.dtype)]
        + [line] * 4
        + [pltpu.VMEM((chunks // 2, part, cols), partial.dtype)]
        + [dma((chunks,))] * 2
        + [dma((tensor, chunks))] * 4
        + [dma((chunks // 2,))] * 2,
        collective_id,
        partial.reshape(2, chunks, part, half * cols),
    ).reshape(-1, cols)


def fast_layer(act, gain, weights, index_all, lengths, cache, newest, active, ids, tensor):
    wq, wo, q_down, q_up, o_down, o_up = weights
    d = lax.axis_index("dp")
    all_rows, k_half = act.shape
    rows = all_rows // 2
    adapters, rank = q_up.shape[0], q_up.shape[1]
    head_dim, slots = cache.shape[-1] // 2, cache.shape[1]
    features = k_half * 2
    selector_all = (index_all[:, None] == jnp.arange(adapters, dtype=jnp.float32)[None, :]).astype(jnp.float32)
    selector = lax.dynamic_slice_in_dim(selector_all, d * rows, rows, 0)

    act32 = act.astype(jnp.float32)
    gain_half = lax.dynamic_slice_in_dim(gain, d * k_half, k_half, 0)
    scaled = (act32 * gain_half).astype(jnp.bfloat16)
    squares = jnp.sum(act32 * act32, axis=-1)
    partial = jnp.dot(scaled, wq, preferred_element_type=jnp.float32)
    down_half = lax.dynamic_slice_in_dim(q_down, d * k_half, k_half, 1)
    ranks = jnp.einsum("nk,akr->nar", scaled, down_half, preferred_element_type=jnp.float32)
    ranks = jnp.sum(selector_all[:, :, None] * ranks, axis=1)
    width = ranks.shape[1]
    small = jnp.concatenate([ranks, squares[:, None]], axis=1)
    small = jnp.pad(small, ((0, 0), (0, -small.shape[1] % 8)))
    small = jnp.transpose(small.reshape(2, rows, -1), (0, 2, 1))
    sent = lax.dynamic_slice_in_dim(partial, (1 - d) * rows, rows, 0).astype(jnp.bfloat16)
    came, smalls = exchange(sent, small, active, ids[0], tensor, False)
    own = lax.dynamic_slice_in_dim(partial, d * rows, rows, 0)
    factor = lax.rsqrt((smalls[0, 0, width] + smalls[1, 0, width]) / features + EPSILON)
    rank_vec = (smalls[0, :, :width] + smalls[1, :, :width]).reshape(rank, rows) * factor[None, :]
    rank_vec = rank_vec.T.astype(jnp.bfloat16)
    query = (own + came.astype(jnp.float32)) * factor[:, None] + ADAPTER_SCALE * jnp.dot(
        widen_rank(selector, rank_vec),
        q_up.reshape(adapters * rank, -1),
        preferred_element_type=jnp.float32,
    )
    query = query.astype(jnp.bfloat16).reshape(rows, slots, -1, head_dim)
    attended = attend(query, cache, newest, lengths).reshape(rows, -1)

    rank_every = jnp.einsum("cb,dbm->cdm", attended, o_down, preferred_element_type=jnp.float32)
    rank_part = jnp.sum(selector[:, :, None] * rank_every, axis=1).T
    came, rank_parts = exchange(attended, rank_part[None], active, ids[1], tensor, True)
    first = jnp.where(d == 0, attended, came)
    second = jnp.where(d == 0, came, attended)
    both = jnp.concatenate([first, second], axis=0)
    partial = jnp.dot(both, wo, preferred_element_type=jnp.float32)
    rank_all = jnp.transpose(jnp.sum(rank_parts, axis=1), (0, 2, 1)).reshape(2 * rows, rank).astype(jnp.bfloat16)
    delta = ADAPTER_SCALE * jnp.dot(
        widen_rank(selector_all, rank_all), o_up.reshape(adapters * rank, -1), preferred_element_type=jnp.float32
    )
    return partial, jnp.concatenate([delta] * (tensor // 2), axis=1)


def fast_body(
    residual_input, norm_gain, wq, wo, q_down, q_up, o_down, o_up, cache, newest, adapter_index, lengths
):
    tensor = lax.axis_size("tensor")
    half = tensor // 2
    d, t, p = lax.axis_index("dp"), lax.axis_index("tensor"), lax.axis_index("pipe")
    rows, cols = residual_input.shape
    weights = tuple(w[0] for w in (wq, wo, q_down, q_up, o_down, o_up))
    gain = lax.dynamic_index_in_dim(norm_gain, p, 0, keepdims=False)
    here = ((jnp.arange(half * cols) // cols + d * half) == t)[None, :]

    index = adapter_index.astype(jnp.float32)
    act, index_other = gather_rows(residual_input, jnp.broadcast_to(index, (8, rows)), 0, 0, tensor)
    index_all = jnp.concatenate([jnp.where(d == 0, index, index_other[0]), jnp.where(d == 0, index_other[0], index)])

    def layer(act, active, ids):
        return fast_layer(act, gain, weights, index_all, lengths, cache[0], newest[0], active, ids, tensor)

    partial, delta = layer(act, 0, (1, 2))
    partial = jnp.where(here, partial + delta, partial).astype(jnp.bfloat16)
    act = reduce_rows(partial, act, 0, 3, tensor)
    partial, delta = layer(act, 1, (4, 5))
    partial = jnp.where(here, partial + delta + act.astype(jnp.float32), partial).astype(jnp.bfloat16)
    return scatter_rows(partial, 1, 6, tensor)


SPECS = (
    P(("groups", "dp"), "tensor"),
    P(),
    P("pipe", "dp", "tensor"),
    P("pipe", "tensor", "dp"),
    P("pipe", None, None, "tensor"),
    P("pipe", None, None, "tensor"),
    P("pipe", None, "tensor", None),
    P("pipe", None, None, "tensor"),
    P("pipe", ("groups", "dp"), "tensor", None, None),
    P("pipe", ("groups", "dp"), "tensor", None),
    P(("groups", "dp")),
    P(("groups", "dp")),
)


def solution(mesh):
    small = mesh.shape["dp"] == 2 and mesh.shape["tensor"] == 4 and mesh.shape["pipe"] == 2
    return jax.shard_map(
        fast_body if small else body,
        mesh=mesh,
        in_specs=SPECS,
        out_specs=P(("groups", "dp", "pipe"), "tensor"),
        check_vma=False,
    )
```
